32 devices in a mesh: ha: 8 (over z, core), wa: 4 (over y, x).
Axes of the slice: x: 2, y: 2, z: 4, core: 2. Of those that a mesh axis runs over, the one named last changes fastest.
Arguments:
- tokens: bfloat16 [128, 128, 512], P('ha', 'wa'), may hold values from -40 to 40
- cotangent: bfloat16 [128, 128, 512], P('ha', 'wa'), may hold values from -6 to 6
- norm_gain: float32 [512], replicated, may hold values from 0.1 to 1.9
- in_weight: bfloat16 [512, 1536], replicated, may hold values from -0.25 to 0.25
- out_weight: bfloat16 [512, 512], replicated, may hold values from -0.25 to 0.25
- bias_table: float32 [16, 31, 31], replicated, may hold values from -256 to 256
Outputs:
- grad_input: bfloat16 [128, 128, 512], P('ha', 'wa')
- grad_table: float32 [16, 31, 31], replicated
The draws below stay inside these ranges and needn't reach their ends.
All inputs are finite; a program needn't handle non-finite values.
Results may differ from the reference program's by a relative error of at most 0.011.
Values may be sent and summed in bfloat16 or wider, within the bound.
A program may use at most 128 MiB of HBM per device.

```python
import jax
import jax.numpy as jnp
from jax import lax

D = 512
HEADS = 16
HEAD_DIM = 32
WIN = 16
TAB = 31
HI = 128
WI = 128


def draw_tokens(key, part):
    key_noise = jax.random.fold_in(key, 11)
    base_draw = jax.random.normal(key_noise, (HI, WI, D), jnp.float32)
    return jnp.clip(base_draw, -40.0, 40.0).astype(jnp.bfloat16)


def draw_bias_table(key, part):
    key_noise = jax.random.fold_in(key, 21)
    base_draw = jax.random.normal(key_noise, (HEADS, TAB, TAB), jnp.float32)
    return jnp.clip(base_draw, -256.0, 256.0)


def steps_of(own_key, dims, pieces, least, largest):
    gain = 1.0
    for axis_at, shards_of in pieces:
        heights = jax.random.uniform(jax.random.fold_in(jax.random.fold_in(own_key, 6), axis_at), (shards_of,), jnp.float32, least / len(pieces), largest / len(pieces))
        gain = gain * jnp.repeat(jnp.exp(heights), dims[axis_at] // shards_of).reshape((-1,) + (1,) * (len(dims) - 1 - axis_at))
    return gain


def scatter_about(rng, dims, width, reach, cuts=(), dtype=jnp.bfloat16):
    values = jax.random.normal(rng, dims, jnp.float32) * width
    if len(cuts) > 0:
        values = steps_of(rng, dims, cuts, -0.22, 0.18) * values
    return jnp.clip(values, min=-reach, max=reach).astype(dtype)


def setup_inputs(seed: int = 0) -> dict:
    seeds = jax.random.split(jax.random.key(seed), 7)
    return {
        "tokens": draw_tokens(jax.random.fold_in(seeds[6], 71), 0),
        "cotangent": scatter_about(seeds[1], (HI, WI, D), 1.0, 6.0, ((0, 8), (1, 4))),
        "norm_gain": jnp.clip(1.0 + 0.18 * jax.random.normal(seeds[2], (D,), jnp.float32), 0.1, 1.9),
        "in_weight": scatter_about(seeds[3], (D, 3 * D), D ** -0.5, 0.25),
        "out_weight": scatter_about(seeds[4], (D, D), D ** -0.5, 0.25),
        "bias_table": draw_bias_table(jax.random.fold_in(seeds[6], 71), 0),
    }


NORM_EPS = 1e-05

def offset_hot():
    places = jnp.arange(WIN)
    slot_ids = jnp.arange(TAB)
    return (places[:, None, None] - places[None, :, None] + (WIN - 1) == slot_ids[None, None, :]).astype(jnp.float32)

def full_bias(bias_table, offset_table):
    partial_rows = jnp.einsum('abd,hde->habe', offset_table, bias_table, precision=lax.Precision.HIGHEST)
    spread = jnp.einsum('uve,habe->haubv', offset_table, partial_rows, precision=lax.Precision.HIGHEST)
    return spread.reshape(HEADS, WIN * WIN, WIN * WIN)

def group_grad(group_tokens, group_cot, norm_gain, in_weight, out_weight, bias_full, offset_table):
    group_rows = WIN * WIN
    tokens_wide = group_tokens.astype(jnp.float32)
    center = lax.optimization_barrier(jnp.mean(tokens_wide, axis=-1, keepdims=True))
    shifted = tokens_wide - center
    inv_std = lax.rsqrt(lax.optimization_barrier(jnp.mean(shifted * shifted, axis=-1, keepdims=True)) + NORM_EPS)
    unit_rows = shifted * inv_std
    normed = (unit_rows * norm_gain).astype(jnp.bfloat16)
    mixed_rows = jnp.dot(normed, in_weight, preferred_element_type=jnp.float32)
    query_scale = HEAD_DIM ** (-0.5)
    queries = (mixed_rows[:, :D] * query_scale).astype(jnp.bfloat16).reshape(group_rows, HEADS, HEAD_DIM)
    key_rows = mixed_rows[:, D:2 * D].astype(jnp.bfloat16).reshape(group_rows, HEADS, HEAD_DIM)
    values = mixed_rows[:, 2 * D:].astype(jnp.bfloat16).reshape(group_rows, HEADS, HEAD_DIM)
    scores = jnp.einsum('thd,shd->hts', queries.astype(jnp.float32), key_rows.astype(jnp.float32)) + bias_full
    row_top = lax.optimization_barrier(jnp.max(scores, axis=-1, keepdims=True))
    exponent = jnp.exp(scores - row_top)
    attn_probs = exponent / lax.optimization_barrier(jnp.sum(exponent, axis=-1, keepdims=True))
    probs_half = attn_probs.astype(jnp.bfloat16)
    grad_out = lax.dot_general(group_cot, out_weight, (((1,), (1,)), ((), ())), preferred_element_type=jnp.float32)
    grad_out = grad_out.astype(jnp.bfloat16).reshape(group_rows, HEADS, HEAD_DIM)
    grad_probs = jnp.einsum('thd,shd->hts', grad_out.astype(jnp.float32), values.astype(jnp.float32))
    grad_values = jnp.einsum('hts,thd->shd', probs_half.astype(jnp.float32), grad_out.astype(jnp.float32)).astype(jnp.bfloat16)
    grad_scores = attn_probs * (grad_probs - lax.optimization_barrier(jnp.sum(attn_probs * grad_probs, axis=-1, keepdims=True)))
    scores_half = grad_scores.astype(jnp.bfloat16).astype(jnp.float32)
    grad_queries = (jnp.einsum('hts,shd->thd', scores_half, key_rows.astype(jnp.float32)) * query_scale).astype(jnp.bfloat16)
    grad_keys = jnp.einsum('hts,thd->shd', scores_half, queries.astype(jnp.float32)).astype(jnp.bfloat16)
    grad_mixed = jnp.concatenate([grad_queries.reshape(group_rows, D), grad_keys.reshape(group_rows, D), grad_values.reshape(group_rows, D)], axis=1)
    grad_normed = lax.dot_general(grad_mixed, in_weight, (((1,), (1,)), ((), ())), preferred_element_type=jnp.float32)
    grad_unit = grad_normed * norm_gain
    grad_rows = inv_std * (grad_unit - lax.optimization_barrier(jnp.mean(grad_unit, axis=-1, keepdims=True)) - unit_rows * lax.optimization_barrier(jnp.mean(grad_unit * unit_rows, axis=-1, keepdims=True)))
    folded = jnp.einsum('haubv,uve->habe', grad_scores.reshape(HEADS, WIN, WIN, WIN, WIN), offset_table, precision=lax.Precision.HIGHEST)
    table_part = jnp.einsum('habe,abd->hde', folded, offset_table, precision=lax.Precision.HIGHEST)
    return (grad_rows.astype(jnp.bfloat16), table_part)

def reference(tokens, cotangent, norm_gain, in_weight, out_weight, bias_table):
    stride_h = HI // WIN
    stride_w = WI // WIN
    offset_table = offset_hot()
    bias_full = full_bias(bias_table, offset_table)

    def regroup(field):
        return field.reshape(WIN, stride_h, WIN, stride_w, D).transpose(1, 3, 0, 2, 4).reshape(stride_h * stride_w, WIN * WIN, D)

    def group_step(table_total, pair_rows):
        grad_rows, table_part = group_grad(pair_rows[0], pair_rows[1], norm_gain, in_weight, out_weight, bias_full, offset_table)
        return (table_total + table_part, grad_rows)
    table_total, grad_groups = lax.scan(group_step, jnp.zeros((HEADS, TAB, TAB), jnp.float32), (regroup(tokens), regroup(cotangent)))
    grad_input = grad_groups.reshape(stride_h, stride_w, WIN, WIN, D).transpose(2, 0, 3, 1, 4).reshape(HI, WI, D)
    return (grad_input, table_total)
```

```python
import functools

import jax
import jax.numpy as jnp
from jax import lax
from jax.experimental import pallas as pl
from jax.experimental.pallas import tpu as pltpu
from jax.sharding import PartitionSpec as P

D = 512
HEADS = 16
HEAD_DIM = 32
WIN = 16
TAB = 31
ROWS = WIN * WIN
SPAN = 2 * ROWS
LANES = 128
PER_BLOCK = LANES // HEAD_DIM
NORM_EPS = 1e-05
SCALE = HEAD_DIM ** (-0.5)


def nt(a, b):
    return lax.dot_general(a, b, (((1,), (1,)), ((), ())), preferred_element_type=jnp.float32)


def nn(a, b):
    return jnp.dot(a, b, preferred_element_type=jnp.float32)


def skew(rows, sign):
    at_row = lax.broadcasted_iota(jnp.int32, rows.shape, 0)
    for bit in range(4):
        moved = pltpu.roll(rows, (sign * (1 << bit)) % SPAN, 1)
        rows = jnp.where((at_row >> bit) % 2 == 1, moved, rows)
    return rows


def low_half():
    return lax.broadcasted_iota(jnp.int32, (WIN, SPAN), 1) % (2 * WIN) < WIN


def build_bias(tab_ref, bias_ref):
    def head(h, carry):
        pair = tab_ref[h]
        even = skew(jnp.broadcast_to(pair[0:1], (WIN, SPAN)), 1)
        odd = skew(jnp.broadcast_to(pair[1:2], (WIN, SPAN)), 1)
        strip = jnp.where(low_half(), pltpu.roll(even, SPAN - WIN, 1), odd)
        for low in range(8):
            turned = strip if low == 0 else pltpu.roll(strip, SPAN - low * WIN, 1)
            for high in range(2):
                a = WIN - 1 - (8 * high + low)
                bias_ref[h, a * WIN : (a + 1) * WIN, :] = turned[:, high * LANES : high * LANES + ROWS]
        return carry

    lax.fori_loop(0, HEADS, head, 0)


def fold_table(dsum_ref, out_ref):
    def head(h, carry):
        total = jnp.zeros((WIN, SPAN), jnp.float32)
        gap = jnp.zeros((WIN, LANES), jnp.float32)
        for low in range(8):
            first = WIN - 1 - low
            second = first - 8
            near = dsum_ref[h, first * WIN : (first + 1) * WIN, :]
            far = dsum_ref[h, second * WIN : (second + 1) * WIN, :]
            both = jnp.concatenate([near, gap, gap], axis=1) + jnp.concatenate([gap, far, gap], axis=1)
            total = total + (both if low == 0 else pltpu.roll(both, low * WIN, 1))
        low_lanes = low_half()
        even = skew(pltpu.roll(jnp.where(low_lanes, total, 0.0), WIN, 1), -1)
        odd = skew(jnp.where(low_lanes, 0.0, total), -1)
        out_ref[h] = jnp.concatenate(
            [jnp.sum(even, axis=0, keepdims=True), jnp.sum(odd, axis=0, keepdims=True)], axis=0
        )
        return carry

    lax.fori_loop(0, HEADS, head, 0)


def prepare(g, tok, cot, gain, win_ref, wout_ref, s):
    wide = tok.astype(jnp.float32)
    shifted = wide - jnp.mean(wide, axis=-1, keepdims=True)
    inv_std = lax.rsqrt(jnp.mean(shifted * shifted, axis=-1, keepdims=True) + NORM_EPS)
    unit = shifted * inv_std
    s.unit[g] = unit
    s.inv[g] = inv_std
    normed = (unit * gain).astype(jnp.bfloat16)
    queries = (nn(normed, win_ref[:, :D]) * SCALE).astype(jnp.bfloat16)
    s.q[g] = queries
    s.qt[g] = queries.T
    keys = nn(normed, win_ref[:, D : 2 * D]).astype(jnp.bfloat16)
    s.k[g] = keys
    s.kt[g] = keys.T
    s.v[g] = nn(normed, win_ref[:, 2 * D :]).astype(jnp.bfloat16)
    grad_out = nt(cot, wout_ref[...]).astype(jnp.bfloat16)
    s.o[g] = grad_out
    s.ot[g] = grad_out.T


def attend(g, s):
    lane = lax.broadcasted_iota(jnp.int32, (ROWS, LANES), 1) // HEAD_DIM

    def block(i, carry):
        at = pl.ds(pl.multiple_of(i * LANES, LANES), LANES)
        q, k, v, o = s.q[g, :, at], s.k[g, :, at], s.v[g, :, at], s.o[g, :, at]
        for j in range(PER_BLOCK):
            h = i * PER_BLOCK + j
            own = lane == j
            zero = jnp.zeros_like(q)
            scores = nt(jnp.where(own, q, zero), k) + s.bias[h]
            exponent = jnp.exp(scores - jnp.max(scores, axis=-1, keepdims=True))
            probs = exponent * (1.0 / jnp.sum(exponent, axis=-1, keepdims=True))
            grad_probs = nt(jnp.where(own, o, zero), v)
            mean = jnp.sum(probs * grad_probs, axis=-1, keepdims=True)
            grad_scores = probs * (grad_probs - mean)
            if g == 0:
                s.dsum[h] = grad_scores
            else:
                s.dsum[h] += grad_scores
            half = grad_scores.astype(jnp.bfloat16)
            rows = pl.ds(pl.multiple_of(h * HEAD_DIM, HEAD_DIM), HEAD_DIM)
            rows_k = pl.ds(pl.multiple_of(D + h * HEAD_DIM, HEAD_DIM), HEAD_DIM)
            rows_v = pl.ds(pl.multiple_of(2 * D + h * HEAD_DIM, HEAD_DIM), HEAD_DIM)
            s.mixed[rows_v, :] = nn(s.ot[g, rows, :], probs.astype(jnp.bfloat16)).astype(jnp.bfloat16)
            s.mixed[rows_k, :] = nn(s.qt[g, rows, :], half).astype(jnp.bfloat16)
            s.mixed[rows, :] = (nt(s.kt[g, rows, :], half) * SCALE).astype(jnp.bfloat16)
        return carry

    lax.fori_loop(0, HEADS // PER_BLOCK, block, 0)


def finish(g, gain, win_ref, s):
    grad_unit = nn(win_ref[...], s.mixed[...]).T * gain
    unit = s.unit[g]
    inner = grad_unit - jnp.mean(grad_unit, axis=-1, keepdims=True)
    inner = inner - unit * jnp.mean(grad_unit * unit, axis=-1, keepdims=True)
    return (s.inv[g] * inner).astype(jnp.bfloat16)


class Scratch:
    NAMES = ("unit", "inv", "q", "k", "v", "o", "qt", "kt", "ot", "mixed", "bias", "dsum")

    def __init__(self, refs):
        for name, ref in zip(self.NAMES, refs):
            setattr(self, name, ref)

    @staticmethod
    def shapes(groups):
        wide = pltpu.VMEM((groups, ROWS, D), jnp.bfloat16)
        tall = pltpu.VMEM((groups, D, ROWS), jnp.bfloat16)
        square = pltpu.VMEM((HEADS, ROWS, ROWS), jnp.float32)
        return [
            pltpu.VMEM((groups, ROWS, D), jnp.float32),
            pltpu.VMEM((groups, ROWS, 1), jnp.float32),
            wide, wide, wide, wide, tall, tall, tall,
            pltpu.VMEM((3 * D, ROWS), jnp.bfloat16),
            square, square,
        ]


def local_kernel(tok_ref, cot_ref, gain_ref, win_ref, wout_ref, tab_ref, grad_ref, out_ref, *refs):
    s = Scratch(refs)
    build_bias(tab_ref, s.bias)
    gain = gain_ref[...]
    for g in range(tok_ref.shape[0]):
        prepare(g, tok_ref[g], cot_ref[g], gain, win_ref, wout_ref, s)
        attend(g, s)
        grad_ref[g] = finish(g, gain, win_ref, s)
    fold_table(s.dsum, out_ref)


def local_call(tok, cot, gain, w_in, w_out, tab):
    groups = tok.shape[0]
    whole = pl.BlockSpec(memory_space=pltpu.VMEM)
    return pl.pallas_call(
        local_kernel,
        out_shape=(
            jax.ShapeDtypeStruct(tok.shape, jnp.bfloat16),
            jax.ShapeDtypeStruct(tab.shape, jnp.float32),
        ),
        in_specs=[whole] * 6,
        out_specs=(whole, whole),
        scratch_shapes=Scratch.shapes(groups),
        compiler_params=pltpu.CompilerParams(vmem_limit_bytes=48 * 2**20),
        name="grid_attention_grad",
    )(tok, cot, gain, w_in, w_out, tab)


def pack_table(bias_table):
    turned = jnp.flip(bias_table, (1, 2))
    padded = jnp.pad(turned, ((0, 0), (0, 1), (1, 0)))
    return padded.reshape(HEADS, WIN, 2, 2 * WIN).transpose(0, 2, 1, 3).reshape(HEADS, 2, SPAN)


def unpack_table(packed):
    split = packed.reshape(HEADS, 2, WIN, 2 * WIN).transpose(0, 2, 1, 3).reshape(HEADS, 2 * WIN, 2 * WIN)
    return jnp.flip(split[:, :TAB, 1:], (1, 2))


def body(tokens, cotangent, norm_gain, in_weight, out_weight, bias_table):
    high_parts = lax.axis_size("ha")
    wide_parts = lax.axis_size("wa")
    parts = high_parts * wide_parts
    rows_local, cols_local, channels = tokens.shape
    row_steps = WIN // high_parts
    col_steps = WIN // wide_parts
    row_groups = rows_local // row_steps // high_parts
    col_groups = cols_local // col_steps // wide_parts
    groups = row_groups * col_groups

    def send(tile):
        laid = tile.reshape(row_steps, high_parts, row_groups, col_steps, wide_parts, col_groups, channels)
        laid = laid.transpose(1, 4, 2, 5, 0, 3, 6).reshape(parts, groups * row_steps * col_steps, channels)
        got = lax.all_to_all(laid, ("ha", "wa"), split_axis=0, concat_axis=0, tiled=True)
        got = got.reshape(high_parts, wide_parts, groups, row_steps, col_steps, channels)
        return got.transpose(2, 0, 3, 1, 4, 5).reshape(groups, ROWS, channels)

    def back(grads):
        laid = grads.reshape(groups, high_parts, row_steps, wide_parts, col_steps, channels)
        laid = laid.transpose(1, 3, 0, 2, 4, 5).reshape(parts, groups * row_steps * col_steps, channels)
        got = lax.all_to_all(laid, ("ha", "wa"), split_axis=0, concat_axis=0, tiled=True)
        got = got.reshape(high_parts, wide_parts, row_groups, col_groups, row_steps, col_steps, channels)
        return got.transpose(4, 0, 2, 5, 1, 3, 6).reshape(rows_local, cols_local, channels)

    grads, packed = local_call(
        send(tokens), send(cotangent), norm_gain.reshape(1, D), in_weight, out_weight, pack_table(bias_table)
    )
    pieces = packed.reshape(parts, -1)
    pieces = lax.all_to_all(pieces, ("ha", "wa"), split_axis=0, concat_axis=0, tiled=True)
    own = jnp.broadcast_to(jnp.sum(pieces, axis=0, keepdims=True), pieces.shape)
    total = lax.all_to_all(own, ("ha", "wa"), split_axis=0, concat_axis=0, tiled=True)
    return back(grads), unpack_table(total.reshape(HEADS, 2, SPAN))


def solution(mesh):
    tile = P("ha", "wa", None)
    return jax.shard_map(
        body, mesh=mesh, in_specs=(tile, tile, P(), P(), P(), P()), out_specs=(tile, P()), check_vma=False
    )
```

```python
import functools

import jax
import jax.numpy as jnp
from jax import lax
from jax.experimental import pallas as pl
from jax.experimental.pallas import tpu as pltpu
from jax.sharding import PartitionSpec as P

D = 512
HEADS = 16
HEAD_DIM = 32
WIN = 16
TAB = 31
ROWS = WIN * WIN
SPAN = 2 * ROWS
LANES = 128
PER_BLOCK = LANES // HEAD_DIM
CHUNK = 8
NORM_EPS = 1e-05
SCALE = HEAD_DIM ** (-0.5)
MESH = pl.DeviceIdType.MESH


def nt(a, b):
    return lax.dot_general(a, b, (((1,), (1,)), ((), ())), preferred_element_type=jnp.float32)


def nn(a, b):
    return jnp.dot(a, b, preferred_element_type=jnp.float32)


def skew(rows, sign):
    at_row = lax.broadcasted_iota(jnp.int32, rows.shape, 0)
    for bit in range(4):
        moved = pltpu.roll(rows, (sign * (1 << bit)) % SPAN, 1)
        rows = jnp.where((at_row >> bit) % 2 == 1, moved, rows)
    return rows


def low_half():
    return lax.broadcasted_iota(jnp.int32, (WIN, SPAN), 1) % (2 * WIN) < WIN


def build_bias(tab_ref, bias_ref):
    def head(h, carry):
        pair = tab_ref[h]
        even = skew(jnp.broadcast_to(pair[0:1], (WIN, SPAN)), 1)
        odd = skew(jnp.broadcast_to(pair[1:2], (WIN, SPAN)), 1)
        strip = jnp.where(low_half(), pltpu.roll(even, SPAN - WIN, 1), odd)
        for low in range(8):
            turned = strip if low == 0 else pltpu.roll(strip, SPAN - low * WIN, 1)
            for high in range(2):
                a = WIN - 1 - (8 * high + low)
                bias_ref[h, a * WIN : (a + 1) * WIN, :] = turned[:, high * LANES : high * LANES + ROWS]
        return carry

    lax.fori_loop(0, HEADS, head, 0)


def fold_table(dsum_ref, out_ref):
    def head(h, carry):
        total = jnp.zeros((WIN, SPAN), jnp.float32)
        gap = jnp.zeros((WIN, LANES), jnp.float32)
        for low in range(8):
            first = WIN - 1 - low
            second = first - 8
            near = dsum_ref[h, first * WIN : (first + 1) * WIN, :]
            far = dsum_ref[h, second * WIN : (second + 1) * WIN, :]
            both = jnp.concatenate([near, gap, gap], axis=1) + jnp.concatenate([gap, far, gap], axis=1)
            total = total + (both if low == 0 else pltpu.roll(both, low * WIN, 1))
        low_lanes = low_half()
        even = skew(pltpu.roll(jnp.where(low_lanes, total, 0.0), WIN, 1), -1)
        odd = skew(jnp.where(low_lanes, 0.0, total), -1)
        for parity, rows in enumerate((even, odd)):
            row = jnp.sum(rows, axis=0, keepdims=True)
            for k in range(SPAN // LANES):
                out_ref[2 * h + parity, k : k + 1, :] = row[:, k * LANES : (k + 1) * LANES]
        return carry

    lax.fori_loop(0, HEADS, head, 0)


def prepare(g, tok, cot, gain, win_ref, wout_ref, s):
    wide = tok.astype(jnp.float32)
    shifted = wide - jnp.mean(wide, axis=-1, keepdims=True)
    inv_std = lax.rsqrt(jnp.mean(shifted * shifted, axis=-1, keepdims=True) + NORM_EPS)
    unit = shifted * inv_std
    s.unit[g] = unit
    s.inv[g] = inv_std
    normed = (unit * gain).astype(jnp.bfloat16)
    queries = (nn(normed, win_ref[:, :D]) * SCALE).astype(jnp.bfloat16)
    s.q[g] = queries
    s.qt[g] = queries.T
    keys = nn(normed, win_ref[:, D : 2 * D]).astype(jnp.bfloat16)
    s.k[g] = keys
    s.kt[g] = keys.T
    s.v[g] = nn(normed, win_ref[:, 2 * D :]).astype(jnp.bfloat16)
    grad_out = nt(cot, wout_ref[...]).astype(jnp.bfloat16)
    s.o[g] = grad_out
    s.ot[g] = grad_out.T


def attend(g, s):
    lane = lax.broadcasted_iota(jnp.int32, (ROWS, LANES), 1) // HEAD_DIM

    def block(i, carry):
        at = pl.ds(pl.multiple_of(i * LANES, LANES), LANES)
        q, k, v, o = s.q[g, :, at], s.k[g, :, at], s.v[g, :, at], s.o[g, :, at]
        for j in range(PER_BLOCK):
            h = i * PER_BLOCK + j
            own = lane == j
            zero = jnp.zeros_like(q)
            scores = nt(jnp.where(own, q, zero), k) + s.bias[h]
            exponent = jnp.exp(scores - jnp.max(scores, axis=-1, keepdims=True))
            probs = exponent * (1.0 / jnp.sum(exponent, axis=-1, keepdims=True))
            grad_probs = nt(jnp.where(own, o, zero), v)
            mean = jnp.sum(probs * grad_probs, axis=-1, keepdims=True)
            grad_scores = probs * (grad_probs - mean)
            if g == 0:
                s.dsum[h] = grad_scores
            else:
                s.dsum[h] += grad_scores
            half = grad_scores.astype(jnp.bfloat16)
            rows = pl.ds(pl.multiple_of(h * HEAD_DIM, HEAD_DIM), HEAD_DIM)
            rows_k = pl.ds(pl.multiple_of(D + h * HEAD_DIM, HEAD_DIM), HEAD_DIM)
            rows_v = pl.ds(pl.multiple_of(2 * D + h * HEAD_DIM, HEAD_DIM), HEAD_DIM)
            s.mixed[rows_v, :] = nn(s.ot[g, rows, :], probs.astype(jnp.bfloat16)).astype(jnp.bfloat16)
            s.mixed[rows_k, :] = nn(s.qt[g, rows, :], half).astype(jnp.bfloat16)
            s.mixed[rows, :] = (nt(s.kt[g, rows, :], half) * SCALE).astype(jnp.bfloat16)
        return carry

    lax.fori_loop(0, HEADS // PER_BLOCK, block, 0)


def finish(g, gain, win_ref, s):
    grad_unit = nn(win_ref[...], s.mixed[...]).T * gain
    unit = s.unit[g]
    inner = grad_unit - jnp.mean(grad_unit, axis=-1, keepdims=True)
    inner = inner - unit * jnp.mean(grad_unit * unit, axis=-1, keepdims=True)
    return (s.inv[g] * inner).astype(jnp.bfloat16)


class Scratch:
    NAMES = ("unit", "inv", "q", "k", "v", "o", "qt", "kt", "ot", "mixed", "bias", "dsum")

    def __init__(self, refs):
        for name, ref in zip(self.NAMES, refs):
            setattr(self, name, ref)

    @staticmethod
    def shapes(groups):
        wide = pltpu.VMEM((groups, ROWS, D), jnp.bfloat16)
        tall = pltpu.VMEM((groups, D, ROWS), jnp.bfloat16)
        square = pltpu.VMEM((HEADS, ROWS, ROWS), jnp.float32)
        return [
            pltpu.VMEM((groups, ROWS, D), jnp.float32),
            pltpu.VMEM((groups, ROWS, 1), jnp.float32),
            wide, wide, wide, wide, tall, tall, tall,
            pltpu.VMEM((3 * D, ROWS), jnp.bfloat16),
            square, square,
        ]


def local_kernel(tok_ref, cot_ref, gain_ref, win_ref, wout_ref, tab_ref, grad_ref, out_ref, *refs):
    s = Scratch(refs)
    out_ref[...] = jnp.zeros_like(out_ref)
    build_bias(tab_ref, s.bias)
    gain = gain_ref[...]
    for g in range(tok_ref.shape[0]):
        prepare(g, tok_ref[g], cot_ref[g], gain, win_ref, wout_ref, s)
        attend(g, s)
        grad_ref[g] = finish(g, gain, win_ref, s)
    fold_table(s.dsum, out_ref)


def local_call(tok, cot, gain, w_in, w_out, tab):
    groups = tok.shape[0]
    whole = pl.BlockSpec(memory_space=pltpu.VMEM)
    return pl.pallas_call(
        local_kernel,
        out_shape=(
            jax.ShapeDtypeStruct(tok.shape, jnp.bfloat16),
            jax.ShapeDtypeStruct((2 * HEADS, 8, LANES), jnp.float32),
        ),
        in_specs=[whole] * 6,
        out_specs=(whole, whole),
        scratch_shapes=Scratch.shapes(groups),
        compiler_params=pltpu.CompilerParams(vmem_limit_bytes=48 * 2**20),
        name="grid_attention_grad",
    )(tok, cot, gain, w_in, w_out, tab)


def one_hot(rows, cols, place):
    at = place(lax.broadcasted_iota(jnp.int32, (rows, LANES), 0))
    at = jnp.concatenate([at] * (cols // LANES), axis=1)
    hit = at == lax.broadcasted_iota(jnp.int32, (rows, cols), 1)
    return jnp.where(hit, 1.0, 0.0).astype(jnp.bfloat16)


class Plan:
    def __init__(self, high_parts, wide_parts, rows_local, cols_local):
        self.high, self.wide, self.cols = high_parts, wide_parts, cols_local
        self.parts = high_parts * wide_parts
        self.row_steps, self.col_steps = WIN // high_parts, WIN // wide_parts
        self.stride_h, self.stride_w = rows_local // self.row_steps, cols_local // self.col_steps
        self.row_groups, self.col_groups = self.stride_h // high_parts, self.stride_w // wide_parts
        self.groups = self.row_groups * self.col_groups
        self.chunk = self.row_steps * self.col_steps

    def fits(self):
        return self.chunk == CHUNK and self.parts == 2 * HEADS

    def local_row(self, g, at):
        device, step = at // self.chunk, at % self.chunk
        p, q = device // self.wide, device % self.wide
        r, c = step // self.col_steps, step % self.col_steps
        row = r * self.stride_h + p * self.row_groups + g // self.col_groups
        return row * self.cols + c * self.stride_w + q * self.col_groups + g % self.col_groups

    def chunk_row(self, t):
        i, j = t // WIN, t % WIN
        p, r = i // self.row_steps, i % self.row_steps
        q, c = j // self.col_steps, j % self.col_steps
        return (p * self.wide + q, r * self.col_steps + c)

    def position(self, at):
        device, step = at // self.chunk, at % self.chunk
        i = device // self.wide * self.row_steps + step // self.col_steps
        return i * WIN + device % self.wide * self.col_steps + step % self.col_steps

    def place_local(self, at):
        row, col = at // self.cols, at % self.cols
        r, a = row // self.stride_h, row % self.stride_h
        c, b = col // self.stride_w, col % self.stride_w
        g = a % self.row_groups * self.col_groups + b % self.col_groups
        device = a // self.row_groups * self.wide + b // self.col_groups
        return (g * self.parts + device) * self.chunk + r * self.col_steps + c


def fused_kernel(plan, tok_ref, cot_ref, gain_ref, win_ref, wout_ref, tab_ref, grad_ref, out_ref, *refs):
    (send, recv, back, home, part, mine, pieces, total, send_sem, recv_sem, *rest) = refs
    s = Scratch(rest)
    parts, groups = plan.parts, plan.groups
    me = lax.axis_index("ha") * plan.wide + lax.axis_index("wa")
    tile_rows = tok_ref.shape[0]

    def others(step):
        def one(k, carry):
            device = (me + k) % parts
            step(device, (device // plan.wide, device % plan.wide))
            return carry

        lax.fori_loop(1, parts, one, 0)

    def scatter(source, target, slot, size=None):
        def one(device, coords):
            pltpu.make_async_remote_copy(
                src_ref=source(device), dst_ref=target, send_sem=send_sem.at[slot], recv_sem=recv_sem.at[slot],
                device_id=coords, device_id_type=MESH,
            ).start()

        others(one)

    def wait(ref, sem):
        some = ref.at[pl.ds(0, parts - 1)]
        pltpu.make_async_copy(some, some, sem).wait()

    barrier = pltpu.get_barrier_semaphore()
    others(lambda device, coords: pl.semaphore_signal(barrier, inc=1, device_id=coords, device_id_type=MESH))

    for g in range(groups):
        pick = one_hot(ROWS, tile_rows, functools.partial(plan.local_row, g))
        tok = nn(pick, tok_ref[...]).reshape(parts, CHUNK, D)
        cot = nn(pick, cot_ref[...]).reshape(parts, CHUNK, D)
        send[g] = jnp.concatenate([tok, cot], axis=1).astype(jnp.bfloat16)
        if g == 0:
            pl.semaphore_wait(barrier, parts - 1)
        scatter(lambda device: send.at[g, device], recv.at[g, me], g)

    part[...] = jnp.zeros_like(part)
    build_bias(tab_ref, s.bias)
    gain = gain_ref[...]

    def in_chunks(half):
        def place(t):
            device, step = plan.chunk_row(t)
            return device * (2 * CHUNK) + half * CHUNK + step

        return one_hot(ROWS, 2 * CHUNK * parts, place)

    for g in range(groups):
        wait(recv.at[g], recv_sem.at[g])
        recv[g, me] = send[g, me]
        arrived = recv[g].reshape(2 * CHUNK * parts, D)
        tok = nn(in_chunks(0), arrived)
        cot = nn(in_chunks(1), arrived).astype(jnp.bfloat16)
        prepare(g, tok, cot, gain, win_ref, wout_ref, s)
        attend(g, s)
        grads = nn(one_hot(ROWS, ROWS, plan.position), finish(g, gain, win_ref, s)).reshape(parts, CHUNK, D)
        back[g] = jnp.concatenate([grads[:, :, : D // 2], grads[:, :, D // 2 :]], axis=1).astype(jnp.bfloat16)
        scatter(lambda device: back.at[g, device], home.at[g, me], groups + g)

    fold_table(s.dsum, part)
    rows_slot, all_slot = 2 * groups, 2 * groups + 1
    scatter(lambda device: part.at[device], pieces.at[me], rows_slot)
    wait(pieces, recv_sem.at[rows_slot])
    pieces[me] = part[me]
    mine[...] = jnp.sum(pieces[...], axis=0)
    scatter(lambda device: mine, total.at[me], all_slot)

    for g in range(groups):
        wait(home.at[g], recv_sem.at[groups + g])
        home[g, me] = back[g, me]
    landed = home[...].reshape(groups * parts, 2 * CHUNK, D // 2).astype(jnp.float32)
    landed = jnp.concatenate([landed[:, :CHUNK], landed[:, CHUNK:]], axis=2)
    landed = landed.reshape(tile_rows, D).astype(jnp.bfloat16)
    grad_ref[...] = nn(one_hot(tile_rows, tile_rows, plan.place_local), landed).astype(jnp.bfloat16)

    wait(total, recv_sem.at[all_slot])
    total[me] = mine[...]
    out_ref[...] = total[...]
    for g in range(groups):
        wait(send.at[g], send_sem.at[g])
        wait(back.at[g], send_sem.at[groups + g])
    wait(part, send_sem.at[rows_slot])
    wait(total, send_sem.at[all_slot])


def fused_call(plan, tok, cot, gain, w_in, w_out, tab):
    groups, parts = plan.groups, plan.parts
    whole = pl.BlockSpec(memory_space=pltpu.VMEM)
    inward = pltpu.VMEM((groups, parts, 2 * CHUNK, D), jnp.bfloat16)
    outward = pltpu.VMEM((groups, parts, 2 * CHUNK, D // 2), jnp.bfloat16)
    sums = pltpu.VMEM((parts, 8, LANES), jnp.float32)
    return pl.pallas_call(
        functools.partial(fused_kernel, plan),
        out_shape=(
            jax.ShapeDtypeStruct(tok.shape, jnp.bfloat16),
            jax.ShapeDtypeStruct((parts, 8, LANES), jnp.float32),
        ),
        in_specs=[whole] * 6,
        out_specs=(whole, whole),
        scratch_shapes=[
            inward, inward, outward, outward,
            sums, pltpu.VMEM((8, LANES), jnp.float32), sums, sums,
            pltpu.SemaphoreType.DMA((2 * groups + 2,)),
            pltpu.SemaphoreType.DMA((2 * groups + 2,)),
        ] + Scratch.shapes(groups),
        compiler_params=pltpu.CompilerParams(
            vmem_limit_bytes=48 * 2**20, collective_id=0, has_side_effects=True
        ),
        name="grid_attention_grad_exchange",
    )(tok, cot, gain, w_in, w_out, tab)


def pack_table(bias_table):
    turned = jnp.flip(bias_table, (1, 2))
    padded = jnp.pad(turned, ((0, 0), (0, 1), (1, 0)))
    return padded.reshape(HEADS, WIN, 2, 2 * WIN).transpose(0, 2, 1, 3).reshape(HEADS, 2, SPAN)


def unpack_table(packed):
    split = packed[:, : SPAN // LANES].reshape(HEADS, 2, WIN, 2 * WIN).transpose(0, 2, 1, 3).reshape(HEADS, 2 * WIN, 2 * WIN)
    return jnp.flip(split[:, :TAB, 1:], (1, 2))


def body(tokens, cotangent, norm_gain, in_weight, out_weight, bias_table):
    rows_local, cols_local, channels = tokens.shape
    plan = Plan(lax.axis_size("ha"), lax.axis_size("wa"), rows_local, cols_local)
    shared = (norm_gain.reshape(1, D), in_weight, out_weight, pack_table(bias_table))
    if plan.fits():
        flat = (rows_local * cols_local, channels)
        grads, packed = fused_call(plan, tokens.reshape(flat), cotangent.reshape(flat), *shared)
        return grads.reshape(tokens.shape), unpack_table(packed)

    high_parts, wide_parts, parts = plan.high, plan.wide, plan.parts
    row_steps, col_steps, groups = plan.row_steps, plan.col_steps, plan.groups
    row_groups, col_groups = plan.row_groups, plan.col_groups

    def send(tile):
        laid = tile.reshape(row_steps, high_parts, row_groups, col_steps, wide_parts, col_groups, channels)
        laid = laid.transpose(1, 4, 2, 5, 0, 3, 6).reshape(parts, groups * row_steps * col_steps, channels)
        got = lax.all_to_all(laid, ("ha", "wa"), split_axis=0, concat_axis=0, tiled=True)
        got = got.reshape(high_parts, wide_parts, groups, row_steps, col_steps, channels)
        return got.transpose(2, 0, 3, 1, 4, 5).reshape(groups, ROWS, channels)

    def back(grads):
        laid = grads.reshape(groups, high_parts, row_steps, wide_parts, col_steps, channels)
        laid = laid.transpose(1, 3, 0, 2, 4, 5).reshape(parts, groups * row_steps * col_steps, channels)
        got = lax.all_to_all(laid, ("ha", "wa"), split_axis=0, concat_axis=0, tiled=True)
        got = got.reshape(high_parts, wide_parts, row_groups, col_groups, row_steps, col_steps, channels)
        return got.transpose(4, 0, 2, 5, 1, 3, 6).reshape(rows_local, cols_local, channels)

    grads, packed = local_call(send(tokens), send(cotangent), *shared)
    pieces = packed.reshape(parts, -1)
    pieces = lax.all_to_all(pieces, ("ha", "wa"), split_axis=0, concat_axis=0, tiled=True)
    own = jnp.broadcast_to(jnp.sum(pieces, axis=0, keepdims=True), pieces.shape)
    total = lax.all_to_all(own, ("ha", "wa"), split_axis=0, concat_axis=0, tiled=True)
    return back(grads), unpack_table(total.reshape(packed.shape))


def solution(mesh):
    tile = P("ha", "wa", None)
    return jax.shard_map(
        body, mesh=mesh, in_specs=(tile, tile, P(), P(), P(), P()), out_specs=(tile, P()), check_vma=False
    )
```

```python
import functools

import jax
import jax.numpy as jnp
from jax import lax
from jax.experimental import pallas as pl
from jax.experimental.pallas import tpu as pltpu
from jax.sharding import PartitionSpec as P

D = 512
HEADS = 16
HEAD_DIM = 32
WIN = 16
TAB = 31
ROWS = WIN * WIN
SPAN = 2 * ROWS
LANES = 128
PER_BLOCK = LANES // HEAD_DIM
CHUNK = 8
NORM_EPS = 1e-05
SCALE = HEAD_DIM ** (-0.5)
MESH = pl.DeviceIdType.MESH


def nt(a, b):
    return lax.dot_general(a, b, (((1,), (1,)), ((), ())), preferred_element_type=jnp.float32)


def nn(a, b):
    return jnp.dot(a, b, preferred_element_type=jnp.float32)


def skew(rows, sign):
    at_row = lax.broadcasted_iota(jnp.int32, rows.shape, 0)
    for bit in range(4):
        moved = pltpu.roll(rows, (sign * (1 << bit)) % SPAN, 1)
        rows = jnp.where((at_row >> bit) % 2 == 1, moved, rows)
    return rows


def low_half():
    return lax.broadcasted_iota(jnp.int32, (WIN, SPAN), 1) % (2 * WIN) < WIN


def build_bias(tab_ref, bias_ref):
    def head(h, carry):
        pair = tab_ref[h]
        even = skew(jnp.broadcast_to(pair[0:1], (WIN, SPAN)), 1)
        odd = skew(jnp.broadcast_to(pair[1:2], (WIN, SPAN)), 1)
        strip = jnp.where(low_half(), pltpu.roll(even, SPAN - WIN, 1), odd)
        for low in range(8):
            turned = strip if low == 0 else pltpu.roll(strip, SPAN - low * WIN, 1)
            for high in range(2):
                b = WIN - 1 - (8 * high + low)
                bias_ref[h, b * WIN : (b + 1) * WIN, :] = turned[:, high * LANES : high * LANES + ROWS]
        return carry

    lax.fori_loop(0, HEADS, head, 0)


def fold_head(h, dsum_ref, out_ref):
    total = jnp.zeros((WIN, SPAN), jnp.float32)
    gap = jnp.zeros((WIN, LANES), jnp.float32)
    for low in range(8):
        first = WIN - 1 - low
        second = first - 8
        near = dsum_ref[h, first * WIN : (first + 1) * WIN, :]
        far = dsum_ref[h, second * WIN : (second + 1) * WIN, :]
        both = jnp.concatenate([near, gap, gap], axis=1) + jnp.concatenate([gap, far, gap], axis=1)
        total = total + (both if low == 0 else pltpu.roll(both, low * WIN, 1))
    low_lanes = low_half()
    even = skew(pltpu.roll(jnp.where(low_lanes, total, 0.0), WIN, 1), -1)
    odd = skew(jnp.where(low_lanes, 0.0, total), -1)
    for parity, rows in enumerate((even, odd)):
        row = jnp.sum(rows, axis=0, keepdims=True)
        for k in range(SPAN // LANES):
            out_ref[2 * h + parity, k : k + 1, :] = row[:, k * LANES : (k + 1) * LANES]


def prepare(g, tok, cot, gain, win_ref, wout_ref, s):
    wide = tok.astype(jnp.float32)
    shifted = wide - jnp.mean(wide, axis=-1, keepdims=True)
    inv_std = lax.rsqrt(jnp.mean(shifted * shifted, axis=-1, keepdims=True) + NORM_EPS)
    unit = shifted * inv_std
    s.unit[g] = unit
    s.inv[g] = inv_std
    normed = (unit * gain).astype(jnp.bfloat16)
    queries = (nn(normed, win_ref[:, :D]) * SCALE).astype(jnp.bfloat16)
    s.q[g] = queries
    s.qt[g] = queries.T
    keys = nn(normed, win_ref[:, D : 2 * D]).astype(jnp.bfloat16)
    s.k[g] = keys
    s.kt[g] = keys.T
    s.v[g] = nn(normed, win_ref[:, 2 * D :]).astype(jnp.bfloat16)
    grad_out = nt(cot, wout_ref[...]).astype(jnp.bfloat16)
    s.o[g] = grad_out
    s.ot[g] = grad_out.T


def attend(g, last, s, table_ref):
    lane = lax.broadcasted_iota(jnp.int32, (ROWS, LANES), 1) // HEAD_DIM

    def block(i, carry):
        at = pl.ds(pl.multiple_of(i * LANES, LANES), LANES)
        q, k, v, o = s.q[g, :, at], s.k[g, :, at], s.v[g, :, at], s.o[g, :, at]
        qt, ot = s.qt[g, at, :], s.ot[g, at, :]
        zero = jnp.zeros_like(q)
        for j in range(PER_BLOCK):
            h = i * PER_BLOCK + j
            own = lane == j
            scores = nn(jnp.where(own, k, zero), qt) + s.bias[h]
            exponent = jnp.exp(scores - jnp.max(scores, axis=0, keepdims=True))
            probs = exponent * (1.0 / jnp.sum(exponent, axis=0, keepdims=True))
            grad_probs = nn(jnp.where(own, v, zero), ot)
            mean = jnp.sum(probs * grad_probs, axis=0, keepdims=True)
            grad_scores = probs * (grad_probs - mean)
            if g == 0:
                s.dsum[h] = grad_scores
            else:
                s.dsum[h] += grad_scores
            half = grad_scores.astype(jnp.bfloat16)
            s.probs[:, j * ROWS : (j + 1) * ROWS] = probs.astype(jnp.bfloat16)
            s.grads[:, j * ROWS : (j + 1) * ROWS] = half
            s.own_o[j * ROWS : (j + 1) * ROWS, :] = jnp.where(own, o, zero)
            s.own_q[j * ROWS : (j + 1) * ROWS, :] = jnp.where(own, q, zero)
            rows = pl.ds(pl.multiple_of(h * HEAD_DIM, HEAD_DIM), HEAD_DIM)
            s.mixed_q[rows, :] = (nn(s.kt[g, rows, :], half) * SCALE).astype(jnp.bfloat16)
            if last:
                fold_head(h, s.dsum, table_ref)
        at_v = pl.ds(pl.multiple_of(D + i * LANES, LANES), LANES)
        s.mixed[:, at] = nn(s.grads[...], s.own_q[...]).astype(jnp.bfloat16)
        s.mixed[:, at_v] = nn(s.probs[...], s.own_o[...]).astype(jnp.bfloat16)
        return carry

    lax.fori_loop(0, HEADS // PER_BLOCK, block, 0)


def finish(g, gain, win_ref, s):
    grad_normed = nt(s.mixed_q[...].T, win_ref[:, :D]) + nt(s.mixed[...], win_ref[:, D:])
    grad_unit = grad_normed * gain
    unit = s.unit[g]
    inner = grad_unit - jnp.mean(grad_unit, axis=-1, keepdims=True)
    inner = inner - unit * jnp.mean(grad_unit * unit, axis=-1, keepdims=True)
    return (s.inv[g] * inner).astype(jnp.bfloat16)


class Scratch:
    NAMES = ("unit", "inv", "q", "k", "v", "o", "qt", "kt", "ot", "mixed", "mixed_q",
             "probs", "grads", "own_o", "own_q", "bias", "dsum")

    def __init__(self, refs):
        for name, ref in zip(self.NAMES, refs):
            setattr(self, name, ref)

    @staticmethod
    def shapes(groups):
        wide = pltpu.VMEM((groups, ROWS, D), jnp.bfloat16)
        tall = pltpu.VMEM((groups, D, ROWS), jnp.bfloat16)
        square = pltpu.VMEM((HEADS, ROWS, ROWS), jnp.float32)
        return [
            pltpu.VMEM((groups, ROWS, D), jnp.float32),
            pltpu.VMEM((groups, ROWS, 1), jnp.float32),
            wide, wide, wide, wide, tall, tall, tall,
            pltpu.VMEM((ROWS, 2 * D), jnp.bfloat16),
            pltpu.VMEM((D, ROWS), jnp.bfloat16),
            pltpu.VMEM((ROWS, PER_BLOCK * ROWS), jnp.bfloat16),
            pltpu.VMEM((ROWS, PER_BLOCK * ROWS), jnp.bfloat16),
            pltpu.VMEM((PER_BLOCK * ROWS, LANES), jnp.bfloat16),
            pltpu.VMEM((PER_BLOCK * ROWS, LANES), jnp.bfloat16),
            square, square,
        ]


def local_kernel(tok_ref, cot_ref, gain_ref, win_ref, wout_ref, tab_ref, grad_ref, out_ref, *refs):
    s = Scratch(refs)
    out_ref[...] = jnp.zeros_like(out_ref)
    build_bias(tab_ref, s.bias)
    gain = gain_ref[...]
    for g in range(tok_ref.shape[0]):
        prepare(g, tok_ref[g], cot_ref[g], gain, win_ref, wout_ref, s)
        attend(g, g == tok_ref.shape[0] - 1, s, out_ref)
        grad_ref[g] = finish(g, gain, win_ref, s)


def local_call(tok, cot, gain, w_in, w_out, tab):
    groups = tok.shape[0]
    whole = pl.BlockSpec(memory_space=pltpu.VMEM)
    return pl.pallas_call(
        local_kernel,
        out_shape=(
            jax.ShapeDtypeStruct(tok.shape, jnp.bfloat16),
            jax.ShapeDtypeStruct((2 * HEADS, 8, LANES), jnp.float32),
        ),
        in_specs=[whole] * 6,
        out_specs=(whole, whole),
        scratch_shapes=Scratch.shapes(groups),
        compiler_params=pltpu.CompilerParams(vmem_limit_bytes=48 * 2**20),
        name="grid_attention_grad",
    )(tok, cot, gain, w_in, w_out, tab)


def one_hot(rows, cols, place):
    at = place(lax.broadcasted_iota(jnp.int32, (rows, LANES), 0))
    at = jnp.concatenate([at] * (cols // LANES), axis=1)
    hit = at == lax.broadcasted_iota(jnp.int32, (rows, cols), 1)
    return jnp.where(hit, 1.0, 0.0).astype(jnp.bfloat16)


class Plan:
    def __init__(self, high_parts, wide_parts, rows_local, cols_local):
        self.high, self.wide, self.cols = high_parts, wide_parts, cols_local
        self.parts = high_parts * wide_parts
        self.row_steps, self.col_steps = WIN // high_parts, WIN // wide_parts
        self.stride_h, self.stride_w = rows_local // self.row_steps, cols_local // self.col_steps
        self.row_groups, self.col_groups = self.stride_h // high_parts, self.stride_w // wide_parts
        self.groups = self.row_groups * self.col_groups
        self.chunk = self.row_steps * self.col_steps

    def fits(self):
        return self.chunk == CHUNK and self.parts == 2 * HEADS

    def local_row(self, g, at):
        device, step = at // self.chunk, at % self.chunk
        p, q = device // self.wide, device % self.wide
        r, c = step // self.col_steps, step % self.col_steps
        row = r * self.stride_h + p * self.row_groups + g // self.col_groups
        return row * self.cols + c * self.stride_w + q * self.col_groups + g % self.col_groups

    def chunk_row(self, t):
        i, j = t // WIN, t % WIN
        p, r = i // self.row_steps, i % self.row_steps
        q, c = j // self.col_steps, j % self.col_steps
        return (p * self.wide + q, r * self.col_steps + c)

    def position(self, at):
        device, step = at // self.chunk, at % self.chunk
        i = device // self.wide * self.row_steps + step // self.col_steps
        return i * WIN + device % self.wide * self.col_steps + step % self.col_steps

    def place_local(self, at):
        row, col = at // self.cols, at % self.cols
        r, a = row // self.stride_h, row % self.stride_h
        c, b = col // self.stride_w, col % self.stride_w
        g = a % self.row_groups * self.col_groups + b % self.col_groups
        device = a // self.row_groups * self.wide + b // self.col_groups
        return (g * self.parts + device) * self.chunk + r * self.col_steps + c


def fused_kernel(plan, tok_hbm, cot_hbm, gain_ref, win_hbm, wout_hbm, tab_ref, grad_ref, out_ref, *refs):
    tok_ref, cot_ref, win_ref, wout_ref, load_sem, *refs = refs
    (send, recv, back, home, part, mine, pieces, total, send_sem, recv_sem, *rest) = refs
    loads = [
        pltpu.make_async_copy(source, target, load_sem.at[k])
        for k, (source, target) in enumerate(
            ((tok_hbm, tok_ref), (cot_hbm, cot_ref), (win_hbm, win_ref), (wout_hbm, wout_ref))
        )
    ]
    for load in loads:
        load.start()
    s = Scratch(rest)
    parts, groups = plan.parts, plan.groups
    me = lax.axis_index("ha") * plan.wide + lax.axis_index("wa")
    tile_rows = tok_ref.shape[0]

    def others(step):
        def one(k, carry):
            device = (me + k) % parts
            step(device, (device // plan.wide, device % plan.wide))
            return carry

        lax.fori_loop(1, parts, one, 0)

    def scatter(source, target, slot):
        def one(device, coords):
            pltpu.make_async_remote_copy(
                src_ref=source(device), dst_ref=target, send_sem=send_sem.at[slot], recv_sem=recv_sem.at[slot],
                device_id=coords, device_id_type=MESH,
            ).start()

        others(one)

    def wait(ref, sem):
        some = ref.at[pl.ds(0, parts - 1)]
        pltpu.make_async_copy(some, some, sem).wait()

    barrier = pltpu.get_barrier_semaphore()
    others(lambda device, coords: pl.semaphore_signal(barrier, inc=1, device_id=coords, device_id_type=MESH))

    loads[0].wait()
    loads[1].wait()
    for g in range(groups):
        pick = one_hot(ROWS, tile_rows, functools.partial(plan.local_row, g))
        tok = nn(pick, tok_ref[...]).reshape(parts, CHUNK, D)
        cot = nn(pick, cot_ref[...]).reshape(parts, CHUNK, D)
        send[g] = jnp.concatenate([tok, cot], axis=1).astype(jnp.bfloat16)
        if g == 0:
            pl.semaphore_wait(barrier, parts - 1)
        scatter(lambda device: send.at[g, device], recv.at[g, me], g)

    part[...] = jnp.zeros_like(part)
    build_bias(tab_ref, s.bias)
    gain = gain_ref[...]
    loads[2].wait()
    loads[3].wait()
    rows_slot, all_slot = 2 * groups, 2 * groups + 1

    def in_chunks(half):
        def place(t):
            device, step = plan.chunk_row(t)
            return device * (2 * CHUNK) + half * CHUNK + step

        return one_hot(ROWS, 2 * CHUNK * parts, place)

    for g in range(groups):
        wait(recv.at[g], recv_sem.at[g])
        recv[g, me] = send[g, me]
        arrived = recv[g].reshape(2 * CHUNK * parts, D)
        tok = nn(in_chunks(0), arrived)
        cot = nn(in_chunks(1), arrived).astype(jnp.bfloat16)
        prepare(g, tok, cot, gain, win_ref, wout_ref, s)
        attend(g, g == groups - 1, s, part)
        if g == groups - 1:
            scatter(lambda device: part.at[device], pieces.at[me], rows_slot)
        grads = nn(one_hot(ROWS, ROWS, plan.position), finish(g, gain, win_ref, s)).reshape(parts, CHUNK, D)
        back[g] = jnp.concatenate([grads[:, :, : D // 2], grads[:, :, D // 2 :]], axis=1).astype(jnp.bfloat16)
        scatter(lambda device: back.at[g, device], home.at[g, me], groups + g)

    wait(pieces, recv_sem.at[rows_slot])
    pieces[me] = part[me]
    mine[...] = jnp.sum(pieces[...], axis=0)
    scatter(lambda device: mine, total.at[me], all_slot)

    for g in range(groups):
        wait(home.at[g], recv_sem.at[groups + g])
        home[g, me] = back[g, me]
    landed = home[...].reshape(groups * parts, 2 * CHUNK, D // 2).astype(jnp.float32)
    landed = jnp.concatenate([landed[:, :CHUNK], landed[:, CHUNK:]], axis=2)
    landed = landed.reshape(tile_rows, D).astype(jnp.bfloat16)
    grad_ref[...] = nn(one_hot(tile_rows, tile_rows, plan.place_local), landed).astype(jnp.bfloat16)

    wait(total, recv_sem.at[all_slot])
    total[me] = mine[...]
    out_ref[...] = total[...]
    for g in range(groups):
        wait(send.at[g], send_sem.at[g])
        wait(back.at[g], send_sem.at[groups + g])
    wait(part, send_sem.at[rows_slot])
    wait(total, send_sem.at[all_slot])


def fused_call(plan, tok, cot, gain, w_in, w_out, tab):
    groups, parts = plan.groups, plan.parts
    whole = pl.BlockSpec(memory_space=pltpu.VMEM)
    apart = pl.BlockSpec(memory_space=pl.ANY)
    inward = pltpu.VMEM((groups, parts, 2 * CHUNK, D), jnp.bfloat16)
    outward = pltpu.VMEM((groups, parts, 2 * CHUNK, D // 2), jnp.bfloat16)
    sums = pltpu.VMEM((parts, 8, LANES), jnp.float32)
    return pl.pallas_call(
        functools.partial(fused_kernel, plan),
        out_shape=(
            jax.ShapeDtypeStruct(tok.shape, jnp.bfloat16),
            jax.ShapeDtypeStruct((parts, 8, LANES), jnp.float32),
        ),
        in_specs=[apart, apart, whole, apart, apart, whole],
        out_specs=(whole, whole),
        scratch_shapes=[pltpu.VMEM(x.shape, x.dtype) for x in (tok, cot, w_in, w_out)] + [
            pltpu.SemaphoreType.DMA((4,)),
            inward, inward, outward, outward,
            sums, pltpu.VMEM((8, LANES), jnp.float32), sums, sums,
            pltpu.SemaphoreType.DMA((2 * groups + 2,)),
            pltpu.SemaphoreType.DMA((2 * groups + 2,)),
        ] + Scratch.shapes(groups),
        compiler_params=pltpu.CompilerParams(
            vmem_limit_bytes=60 * 2**20, collective_id=0, has_side_effects=True
        ),
        name="grid_attention_grad_exchange",
    )(tok, cot, gain, w_in, w_out, tab)


def pack_table(bias_table):
    padded = jnp.pad(bias_table, ((0, 0), (0, 1), (1, 0)))
    return padded.reshape(HEADS, WIN, 2, 2 * WIN).transpose(0, 2, 1, 3).reshape(HEADS, 2, SPAN)


def unpack_table(packed):
    split = packed[:, : SPAN // LANES].reshape(HEADS, 2, WIN, 2 * WIN).transpose(0, 2, 1, 3).reshape(HEADS, 2 * WIN, 2 * WIN)
    return split[:, :TAB, 1:]


def body(tokens, cotangent, norm_gain, in_weight, out_weight, bias_table):
    rows_local, cols_local, channels = tokens.shape
    plan = Plan(lax.axis_size("ha"), lax.axis_size("wa"), rows_local, cols_local)
    shared = (norm_gain.reshape(1, D), in_weight, out_weight, pack_table(bias_table))
    if plan.fits():
        flat = (rows_local * cols_local, channels)
        grads, packed = fused_call(plan, tokens.reshape(flat), cotangent.reshape(flat), *shared)
        return grads.reshape(tokens.shape), unpack_table(packed)

    high_parts, wide_parts, parts = plan.high, plan.wide, plan.parts
    row_steps, col_steps, groups = plan.row_steps, plan.col_steps, plan.groups
    row_groups, col_groups = plan.row_groups, plan.col_groups

    def send(tile):
        laid = tile.reshape(row_steps, high_parts, row_groups, col_steps, wide_parts, col_groups, channels)
        laid = laid.transpose(1, 4, 2, 5, 0, 3, 6).reshape(parts, groups * row_steps * col_steps, channels)
        got = lax.all_to_all(laid, ("ha", "wa"), split_axis=0, concat_axis=0, tiled=True)
        got = got.reshape(high_parts, wide_parts, groups, row_steps, col_steps, channels)
        return got.transpose(2, 0, 3, 1, 4, 5).reshape(groups, ROWS, channels)

    def back(grads):
        laid = grads.reshape(groups, high_parts, row_steps, wide_parts, col_steps, channels)
        laid = laid.transpose(1, 3, 0, 2, 4, 5).reshape(parts, groups * row_steps * col_steps, channels)
        got = lax.all_to_all(laid, ("ha", "wa"), split_axis=0, concat_axis=0, tiled=True)
        got = got.reshape(high_parts, wide_parts, row_groups, col_groups, row_steps, col_steps, channels)
        return got.transpose(4, 0, 2, 5, 1, 3, 6).reshape(rows_local, cols_local, channels)

    grads, packed = local_call(send(tokens), send(cotangent), *shared)
    pieces = packed.reshape(parts, -1)
    pieces = lax.all_to_all(pieces, ("ha", "wa"), split_axis=0, concat_axis=0, tiled=True)
    own = jnp.broadcast_to(jnp.sum(pieces, axis=0, keepdims=True), pieces.shape)
    total = lax.all_to_all(own, ("ha", "wa"), split_axis=0, concat_axis=0, tiled=True)
    return back(grads), unpack_table(total.reshape(packed.shape))


def solution(mesh):
    tile = P("ha", "wa", None)
    return jax.shard_map(
        body, mesh=mesh, in_specs=(tile, tile, P(), P(), P(), P()), out_specs=(tile, P()), check_vma=False
    )
```

```python
import functools

import jax
import jax.numpy as jnp
from jax import lax
from jax.experimental import pallas as pl
from jax.experimental.pallas import tpu as pltpu
from jax.sharding import PartitionSpec as P

D = 512
HEADS = 16
HEAD_DIM = 32
WIN = 16
TAB = 31
ROWS = WIN * WIN
SPAN = 2 * ROWS
LANES = 128
PER_BLOCK = LANES // HEAD_DIM
CHUNK = 8
STRIDE = 13
NORM_EPS = 1e-05
SCALE = HEAD_DIM ** (-0.5)
MESH = pl.DeviceIdType.MESH


def nt(a, b):
    return lax.dot_general(a, b, (((1,), (1,)), ((), ())), preferred_element_type=jnp.float32)


def nn(a, b):
    return jnp.dot(a, b, preferred_element_type=jnp.float32)


def skew(rows, sign):
    at_row = lax.broadcasted_iota(jnp.int32, rows.shape, 0)
    for bit in range(4):
        moved = pltpu.roll(rows, (sign * (1 << bit)) % SPAN, 1)
        rows = jnp.where((at_row >> bit) % 2 == 1, moved, rows)
    return rows


def low_half():
    return lax.broadcasted_iota(jnp.int32, (WIN, SPAN), 1) % (2 * WIN) < WIN


def build_bias(tab_ref, bias_ref):
    def head(h, carry):
        pair = tab_ref[h]
        even = skew(jnp.broadcast_to(pair[0:1], (WIN, SPAN)), 1)
        odd = skew(jnp.broadcast_to(pair[1:2], (WIN, SPAN)), 1)
        strip = jnp.where(low_half(), pltpu.roll(even, SPAN - WIN, 1), odd)
        for low in range(8):
            turned = strip if low == 0 else pltpu.roll(strip, SPAN - low * WIN, 1)
            for high in range(2):
                b = WIN - 1 - (8 * high + low)
                bias_ref[h, b * WIN : (b + 1) * WIN, :] = turned[:, high * LANES : high * LANES + ROWS]
        return carry

    lax.fori_loop(0, HEADS, head, 0)


def fold_head(h, dsum_ref, out_ref):
    total = jnp.zeros((WIN, SPAN), jnp.float32)
    gap = jnp.zeros((WIN, LANES), jnp.float32)
    for low in range(8):
        first = WIN - 1 - low
        second = first - 8
        near = dsum_ref[h, first * WIN : (first + 1) * WIN, :]
        far = dsum_ref[h, second * WIN : (second + 1) * WIN, :]
        both = jnp.concatenate([near, gap, gap], axis=1) + jnp.concatenate([gap, far, gap], axis=1)
        total = total + (both if low == 0 else pltpu.roll(both, low * WIN, 1))
    low_lanes = low_half()
    even = skew(pltpu.roll(jnp.where(low_lanes, total, 0.0), WIN, 1), -1)
    odd = skew(jnp.where(low_lanes, 0.0, total), -1)
    for parity, rows in enumerate((even, odd)):
        row = jnp.sum(rows, axis=0, keepdims=True)
        for k in range(SPAN // LANES):
            out_ref[2 * h + parity, k : k + 1, :] = row[:, k * LANES : (k + 1) * LANES]


def prepare(g, tok, cot, gain, win_ref, wout_ref, s):
    wide = tok.astype(jnp.float32)
    shifted = wide - jnp.mean(wide, axis=-1, keepdims=True)
    inv_std = lax.rsqrt(jnp.mean(shifted * shifted, axis=-1, keepdims=True) + NORM_EPS)
    unit = shifted * inv_std
    s.unit[g] = unit
    s.inv[g] = inv_std
    normed = (unit * gain).astype(jnp.bfloat16)
    queries = (nn(normed, win_ref[:, :D]) * SCALE).astype(jnp.bfloat16)
    s.q[g] = queries
    s.qt[g] = queries.T
    keys = nn(normed, win_ref[:, D : 2 * D]).astype(jnp.bfloat16)
    s.k[g] = keys
    s.kt[g] = keys.T
    s.v[g] = nn(normed, win_ref[:, 2 * D :]).astype(jnp.bfloat16)
    grad_out = nt(cot, wout_ref[...]).astype(jnp.bfloat16)
    s.o[g] = grad_out
    s.ot[g] = grad_out.T


def attend(g, last, s, table_ref):
    lane = lax.broadcasted_iota(jnp.int32, (ROWS, LANES), 1) // HEAD_DIM

    def block(i, carry):
        at = pl.ds(pl.multiple_of(i * LANES, LANES), LANES)
        q, k, v, o = s.q[g, :, at], s.k[g, :, at], s.v[g, :, at], s.o[g, :, at]
        qt, ot = s.qt[g, at, :], s.ot[g, at, :]
        zero = jnp.zeros_like(q)
        for j in range(PER_BLOCK):
            h = i * PER_BLOCK + j
            own = lane == j
            scores = nn(jnp.where(own, k, zero), qt) + s.bias[h]
            exponent = jnp.exp(scores - jnp.max(scores, axis=0, keepdims=True))
            probs = exponent * (1.0 / jnp.sum(exponent, axis=0, keepdims=True))
            grad_probs = nn(jnp.where(own, v, zero), ot)
            mean = jnp.sum(probs * grad_probs, axis=0, keepdims=True)
            grad_scores = probs * (grad_probs - mean)
            if g == 0:
                s.dsum[h] = grad_scores
            else:
                s.dsum[h] += grad_scores
            half = grad_scores.astype(jnp.bfloat16)
            s.probs[:, j * ROWS : (j + 1) * ROWS] = probs.astype(jnp.bfloat16)
            s.grads[:, j * ROWS : (j + 1) * ROWS] = half
            s.own_o[j * ROWS : (j + 1) * ROWS, :] = jnp.where(own, o, zero)
            s.own_q[j * ROWS : (j + 1) * ROWS, :] = jnp.where(own, q, zero)
            rows = pl.ds(pl.multiple_of(h * HEAD_DIM, HEAD_DIM), HEAD_DIM)
            s.mixed_q[rows, :] = (nn(s.kt[g, rows, :], half) * SCALE).astype(jnp.bfloat16)
            if last:
                fold_head(h, s.dsum, table_ref)
        at_v = pl.ds(pl.multiple_of(D + i * LANES, LANES), LANES)
        s.mixed[:, at] = nn(s.grads[...], s.own_q[...]).astype(jnp.bfloat16)
        s.mixed[:, at_v] = nn(s.probs[...], s.own_o[...]).astype(jnp.bfloat16)
        return carry

    lax.fori_loop(0, HEADS // PER_BLOCK, block, 0)


def finish(g, gain, win_ref, s):
    grad_normed = nt(s.mixed_q[...].T, win_ref[:, :D]) + nt(s.mixed[...], win_ref[:, D:])
    grad_unit = grad_normed * gain
    unit = s.unit[g]
    inner = grad_unit - jnp.mean(grad_unit, axis=-1, keepdims=True)
    inner = inner - unit * jnp.mean(grad_unit * unit, axis=-1, keepdims=True)
    return (s.inv[g] * inner).astype(jnp.bfloat16)


class Scratch:
    NAMES = ("unit", "inv", "q", "k", "v", "o", "qt", "kt", "ot", "mixed", "mixed_q",
             "probs", "grads", "own_o", "own_q", "bias", "dsum")

    def __init__(self, refs):
        for name, ref in zip(self.NAMES, refs):
            setattr(self, name, ref)

    @staticmethod
    def shapes(groups):
        wide = pltpu.VMEM((groups, ROWS, D), jnp.bfloat16)
        tall = pltpu.VMEM((groups, D, ROWS), jnp.bfloat16)
        square = pltpu.VMEM((HEADS, ROWS, ROWS), jnp.float32)
        return [
            pltpu.VMEM((groups, ROWS, D), jnp.float32),
            pltpu.VMEM((groups, ROWS, 1), jnp.float32),
            wide, wide, wide, wide, tall, tall, tall,
            pltpu.VMEM((ROWS, 2 * D), jnp.bfloat16),
            pltpu.VMEM((D, ROWS), jnp.bfloat16),
            pltpu.VMEM((ROWS, PER_BLOCK * ROWS), jnp.bfloat16),
            pltpu.VMEM((ROWS, PER_BLOCK * ROWS), jnp.bfloat16),
            pltpu.VMEM((PER_BLOCK * ROWS, LANES), jnp.bfloat16),
            pltpu.VMEM((PER_BLOCK * ROWS, LANES), jnp.bfloat16),
            square, square,
        ]


def local_kernel(tok_ref, cot_ref, gain_ref, win_ref, wout_ref, tab_ref, grad_ref, out_ref, *refs):
    s = Scratch(refs)
    out_ref[...] = jnp.zeros_like(out_ref)
    build_bias(tab_ref, s.bias)
    gain = gain_ref[...]
    for g in range(tok_ref.shape[0]):
        prepare(g, tok_ref[g], cot_ref[g], gain, win_ref, wout_ref, s)
        attend(g, g == tok_ref.shape[0] - 1, s, out_ref)
        grad_ref[g] = finish(g, gain, win_ref, s)


def local_call(tok, cot, gain, w_in, w_out, tab):
    groups = tok.shape[0]
    whole = pl.BlockSpec(memory_space=pltpu.VMEM)
    return pl.pallas_call(
        local_kernel,
        out_shape=(
            jax.ShapeDtypeStruct(tok.shape, jnp.bfloat16),
            jax.ShapeDtypeStruct((2 * HEADS, 8, LANES), jnp.float32),
        ),
        in_specs=[whole] * 6,
        out_specs=(whole, whole),
        scratch_shapes=Scratch.shapes(groups),
        compiler_params=pltpu.CompilerParams(vmem_limit_bytes=48 * 2**20),
        name="grid_attention_grad",
    )(tok, cot, gain, w_in, w_out, tab)


def one_hot(rows, cols, place):
    at = place(lax.broadcasted_iota(jnp.int32, (rows, LANES), 0))
    at = jnp.concatenate([at] * (cols // LANES), axis=1)
    hit = at == lax.broadcasted_iota(jnp.int32, (rows, cols), 1)
    return jnp.where(hit, 1.0, 0.0).astype(jnp.bfloat16)


class Plan:
    def __init__(self, high_parts, wide_parts, rows_local, cols_local):
        self.high, self.wide, self.cols = high_parts, wide_parts, cols_local
        self.parts = high_parts * wide_parts
        self.row_steps, self.col_steps = WIN // high_parts, WIN // wide_parts
        self.stride_h, self.stride_w = rows_local // self.row_steps, cols_local // self.col_steps
        self.row_groups, self.col_groups = self.stride_h // high_parts, self.stride_w // wide_parts
        self.groups = self.row_groups * self.col_groups
        self.chunk = self.row_steps * self.col_steps

    def fits(self):
        return self.chunk == CHUNK and self.parts == 2 * HEADS

    def local_row(self, g, at):
        device, step = at // self.chunk, at % self.chunk
        p, q = device // self.wide, device % self.wide
        r, c = step // self.col_steps, step % self.col_steps
        row = r * self.stride_h + p * self.row_groups + g // self.col_groups
        return row * self.cols + c * self.stride_w + q * self.col_groups + g % self.col_groups

    def chunk_row(self, t):
        i, j = t // WIN, t % WIN
        p, r = i // self.row_steps, i % self.row_steps
        q, c = j // self.col_steps, j % self.col_steps
        return (p * self.wide + q, r * self.col_steps + c)

    def position(self, at):
        device, step = at // self.chunk, at % self.chunk
        i = device // self.wide * self.row_steps + step // self.col_steps
        return i * WIN + device % self.wide * self.col_steps + step % self.col_steps

    def place_local(self, at):
        row, col = at // self.cols, at % self.cols
        r, a = row // self.stride_h, row % self.stride_h
        c, b = col // self.stride_w, col % self.stride_w
        g = a % self.row_groups * self.col_groups + b % self.col_groups
        device = a // self.row_groups * self.wide + b // self.col_groups
        return (g * self.parts + device) * self.chunk + r * self.col_steps + c


def fused_kernel(plan, tok_hbm, cot_hbm, gain_ref, win_hbm, wout_hbm, tab_ref, grad_ref, out_ref, *refs):
    tok_ref, cot_ref, win_ref, wout_ref, load_sem, *refs = refs
    pick_tok, pick_cot, pick_back, pick_home, *refs = refs
    (send, recv, back, home, part, mine, pieces, total, send_sem, recv_sem, *rest) = refs
    loads = [
        pltpu.make_async_copy(source, target, load_sem.at[k])
        for k, (source, target) in enumerate(
            ((tok_hbm, tok_ref), (cot_hbm, cot_ref), (win_hbm, win_ref), (wout_hbm, wout_ref))
        )
    ]
    for load in loads:
        load.start()
    s = Scratch(rest)
    parts, groups = plan.parts, plan.groups
    me = lax.axis_index("ha") * plan.wide + lax.axis_index("wa")
    tile_rows = tok_ref.shape[0]

    def others(step):
        def one(k, carry):
            device = (me + STRIDE * k) % parts
            step(device, (device // plan.wide, device % plan.wide))
            return carry

        lax.fori_loop(1, parts, one, 0)

    def scatter(source, target, slot):
        def one(device, coords):
            pltpu.make_async_remote_copy(
                src_ref=source(device), dst_ref=target, send_sem=send_sem.at[slot], recv_sem=recv_sem.at[slot],
                device_id=coords, device_id_type=MESH,
            ).start()

        others(one)

    def wait(ref, sem):
        some = ref.at[pl.ds(0, parts - 1)]
        pltpu.make_async_copy(some, some, sem).wait()

    barrier = pltpu.get_barrier_semaphore()
    others(lambda device, coords: pl.semaphore_signal(barrier, inc=1, device_id=coords, device_id_type=MESH))

    loads[0].wait()
    loads[1].wait()
    def send_group(g):
        scatter(lambda device: send.at[g, device], recv.at[g, me], g)

    for g in range(groups):
        pick = one_hot(ROWS, tile_rows, functools.partial(plan.local_row, g))
        tok = nn(pick, tok_ref[...]).reshape(parts, CHUNK, D)
        cot = nn(pick, cot_ref[...]).reshape(parts, CHUNK, D)
        send[g] = jnp.concatenate([tok, cot], axis=1).astype(jnp.bfloat16)
        if g == 0:
            pl.semaphore_wait(barrier, parts - 1)
            send_group(0)

    part[...] = jnp.zeros_like(part)
    build_bias(tab_ref, s.bias)
    gain = gain_ref[...]
    loads[2].wait()
    loads[3].wait()
    rows_slot, all_slot = 2 * groups, 2 * groups + 1

    def in_chunks(half):
        def place(t):
            device, step = plan.chunk_row(t)
            return device * (2 * CHUNK) + half * CHUNK + step

        return one_hot(ROWS, 2 * CHUNK * parts, place)

    pick_tok[...] = in_chunks(0)
    pick_cot[...] = in_chunks(1)
    pick_back[...] = one_hot(ROWS, ROWS, plan.position)
    pick_home[...] = one_hot(tile_rows, tile_rows, plan.place_local)

    for g in range(groups):
        wait(recv.at[g], recv_sem.at[g])
        if g + 1 < groups:
            send_group(g + 1)
        recv[g, me] = send[g, me]
        arrived = recv[g].reshape(2 * CHUNK * parts, D)
        tok = nn(pick_tok[...], arrived)
        cot = nn(pick_cot[...], arrived).astype(jnp.bfloat16)
        prepare(g, tok, cot, gain, win_ref, wout_ref, s)
        attend(g, g == groups - 1, s, part)
        if g == groups - 1:
            scatter(lambda device: part.at[device], pieces.at[me], rows_slot)
        grads = nn(pick_back[...], finish(g, gain, win_ref, s)).reshape(parts, CHUNK, D)
        back[g] = jnp.concatenate([grads[:, :, : D // 2], grads[:, :, D // 2 :]], axis=1).astype(jnp.bfloat16)
        scatter(lambda device: back.at[g, device], home.at[g, me], groups + g)

    wait(pieces, recv_sem.at[rows_slot])
    pieces[me] = part[me]
    mine[...] = jnp.sum(pieces[...], axis=0)
    scatter(lambda device: mine, total.at[me], all_slot)

    for g in range(groups):
        wait(home.at[g], recv_sem.at[groups + g])
        home[g, me] = back[g, me]
    landed = home[...].reshape(groups * parts, 2 * CHUNK, D // 2).astype(jnp.float32)
    landed = jnp.concatenate([landed[:, :CHUNK], landed[:, CHUNK:]], axis=2)
    landed = landed.reshape(tile_rows, D).astype(jnp.bfloat16)
    grad_ref[...] = nn(pick_home[...], landed).astype(jnp.bfloat16)

    wait(total, recv_sem.at[all_slot])
    total[me] = mine[...]
    out_ref[...] = total[:, : SPAN // LANES, :]
    for g in range(groups):
        wait(send.at[g], send_sem.at[g])
        wait(back.at[g], send_sem.at[groups + g])
    wait(part, send_sem.at[rows_slot])
    wait(total, send_sem.at[all_slot])


def fused_call(plan, tok, cot, gain, w_in, w_out, tab):
    groups, parts = plan.groups, plan.parts
    whole = pl.BlockSpec(memory_space=pltpu.VMEM)
    apart = pl.BlockSpec(memory_space=pl.ANY)
    inward = pltpu.VMEM((groups, parts, 2 * CHUNK, D), jnp.bfloat16)
    outward = pltpu.VMEM((groups, parts, 2 * CHUNK, D // 2), jnp.bfloat16)
    sums = pltpu.VMEM((parts, 8, LANES), jnp.float32)
    return pl.pallas_call(
        functools.partial(fused_kernel, plan),
        out_shape=(
            jax.ShapeDtypeStruct(tok.shape, jnp.bfloat16),
            jax.ShapeDtypeStruct((parts, SPAN // LANES, LANES), jnp.float32),
        ),
        in_specs=[apart, apart, whole, apart, apart, whole],
        out_specs=(whole, whole),
        scratch_shapes=[pltpu.VMEM(x.shape, x.dtype) for x in (tok, cot, w_in, w_out)] + [
            pltpu.SemaphoreType.DMA((4,)),
            pltpu.VMEM((ROWS, 2 * CHUNK * parts), jnp.bfloat16),
            pltpu.VMEM((ROWS, 2 * CHUNK * parts), jnp.bfloat16),
            pltpu.VMEM((ROWS, ROWS), jnp.bfloat16),
            pltpu.VMEM((tok.shape[0], tok.shape[0]), jnp.bfloat16),
            inward, inward, outward, outward,
            sums, pltpu.VMEM((8, LANES), jnp.float32), sums, sums,
            pltpu.SemaphoreType.DMA((2 * groups + 2,)),
            pltpu.SemaphoreType.DMA((2 * groups + 2,)),
        ] + Scratch.shapes(groups),
        compiler_params=pltpu.CompilerParams(
            vmem_limit_bytes=60 * 2**20, collective_id=0, has_side_effects=True
        ),
        name="grid_attention_grad_exchange",
    )(tok, cot, gain, w_in, w_out, tab)


def pack_table(bias_table):
    padded = jnp.pad(bias_table, ((0, 0), (0, 1), (1, 0)))
    return padded.reshape(HEADS, WIN, 2, 2 * WIN).transpose(0, 2, 1, 3).reshape(HEADS, 2, SPAN)


def unpack_table(packed):
    split = packed.reshape(HEADS, 2, WIN, 2 * WIN).transpose(0, 2, 1, 3).reshape(HEADS, 2 * WIN, 2 * WIN)
    return split[:, :TAB, 1:]


def body(tokens, cotangent, norm_gain, in_weight, out_weight, bias_table):
    rows_local, cols_local, channels = tokens.shape
    plan = Plan(lax.axis_size("ha"), lax.axis_size("wa"), rows_local, cols_local)
    shared = (norm_gain.reshape(1, D), in_weight, out_weight, pack_table(bias_table))
    if plan.fits():
        flat = (rows_local * cols_local, channels)
        grads, packed = fused_call(plan, tokens.reshape(flat), cotangent.reshape(flat), *shared)
        return grads.reshape(tokens.shape), unpack_table(packed)

    high_parts, wide_parts, parts = plan.high, plan.wide, plan.parts
    row_steps, col_steps, groups = plan.row_steps, plan.col_steps, plan.groups
    row_groups, col_groups = plan.row_groups, plan.col_groups

    def send(tile):
        laid = tile.reshape(row_steps, high_parts, row_groups, col_steps, wide_parts, col_groups, channels)
        laid = laid.transpose(1, 4, 2, 5, 0, 3, 6).reshape(parts, groups * row_steps * col_steps, channels)
        got = lax.all_to_all(laid, ("ha", "wa"), split_axis=0, concat_axis=0, tiled=True)
        got = got.reshape(high_parts, wide_parts, groups, row_steps, col_steps, channels)
        return got.transpose(2, 0, 3, 1, 4, 5).reshape(groups, ROWS, channels)

    def back(grads):
        laid = grads.reshape(groups, high_parts, row_steps, wide_parts, col_steps, channels)
        laid = laid.transpose(1, 3, 0, 2, 4, 5).reshape(parts, groups * row_steps * col_steps, channels)
        got = lax.all_to_all(laid, ("ha", "wa"), split_axis=0, concat_axis=0, tiled=True)
        got = got.reshape(high_parts, wide_parts, row_groups, col_groups, row_steps, col_steps, channels)
        return got.transpose(4, 0, 2, 5, 1, 3, 6).reshape(rows_local, cols_local, channels)

    grads, packed = local_call(send(tokens), send(cotangent), *shared)
    pieces = packed.reshape(parts, -1)
    pieces = lax.all_to_all(pieces, ("ha", "wa"), split_axis=0, concat_axis=0, tiled=True)
    own = jnp.broadcast_to(jnp.sum(pieces, axis=0, keepdims=True), pieces.shape)
    total = lax.all_to_all(own, ("ha", "wa"), split_axis=0, concat_axis=0, tiled=True)
    return back(grads), unpack_table(total.reshape(packed.shape)[:, : SPAN // LANES])


def solution(mesh):
    tile = P("ha", "wa", None)
    return jax.shard_map(
        body, mesh=mesh, in_specs=(tile, tile, P(), P(), P(), P()), out_specs=(tile, P()), check_vma=False
    )
```
